32 devices in a mesh: grp: 2 (over x), trn: 16 (over z, y, core).
Axes of the slice: x: 2, y: 2, z: 4, core: 2. Of those that a mesh axis runs over, the one named last changes fastest.
Arguments:
- train_features: bfloat16 [2, 40960, 2048], P(None, ('grp', 'trn')), parts along dimension 1, may hold values from -6 to 6
- residual_weights: float32 [2, 40960], P(None, ('grp', 'trn')), parts along dimension 1, may hold values from 0.06 to 1, as said below
- target_features: bfloat16 [2, 512, 2048], P(None, ('grp', 'trn')), parts along dimension 1, may hold values from -0.125 to 0.125
Outputs:
- scores: bfloat16 [40960, 256], P(('grp', 'trn')), parts along dimension 0
The draws below stay inside these ranges and needn't reach their ends.
There are 2 independent parts, one for each index of `grp`. The reference program is written for one: setup_inputs(seed, part) draws one part's arguments, and reference() takes and returns one part's arrays. A program takes and returns all parts, laid end to end along the dimension named above; each array names one. Nothing has to cross between parts.
Inputs may be any that keep to these rules, and one draw needn't show every extreme that they name: `residual_weights`: strictly positive weights.
All inputs are finite; a program needn't handle non-finite values.
Results may differ from the reference program's by a relative error of at most 0.0004.
Values may be sent and summed in bfloat16 or wider, within the bound.
A program may use at most 64 MiB of HBM per device.

```python
import jax
import jax.numpy as jnp
from jax import lax

K = 2048
CKPTS = 2
TRAIN = 20480
TARGETS = 256


def draw_residual_weights(key, part):
    key = jax.random.fold_in(key, 7)
    position = jnp.arange(TRAIN, dtype=jnp.float32) / (TRAIN - 1)
    ramp = jnp.exp(jnp.log(3.0) * position) / 3.0
    factor = jax.random.uniform(key, (CKPTS, TRAIN), jnp.float32, 0.2, 1.0)
    return (factor * ramp[None, :]).astype(jnp.float32)


def block_scale(stream_key, shape, split, smallest, top_value):
    gain, own = 1.0, jax.random.fold_in(stream_key, 6)
    for dim, parts in split:
        steps = jnp.exp(jax.random.uniform(jax.random.fold_in(own, dim), (parts,), jnp.float32, smallest / len(split), top_value / len(split)))
        gain = gain * jnp.repeat(steps, shape[dim] // parts).reshape([-1 if axis == dim else 1 for axis in range(len(shape))])
    return gain


def normal_values(key, dims, spread, limit, split=(), held_as=jnp.bfloat16):
    values = spread * jax.random.normal(key, dims, jnp.float32)
    if split:
        values = values * block_scale(key, dims, split, -0.22, 0.18)
    return jnp.clip(values, -limit, limit).astype(held_as)


def setup_inputs(seed: int = 0, part: int = 0) -> dict:
    key_of = jax.random.split(jax.random.key(seed), 4)
    part_keys = jax.random.split(jax.random.fold_in(key_of[3], part), 4)
    return {
        "train_features": normal_values(part_keys[0], (CKPTS, TRAIN, K), 1.0, 6.0, ((1, 16),)),
        "residual_weights": draw_residual_weights(jax.random.fold_in(jax.random.fold_in(key_of[3], part), 71), part),
        "target_features": normal_values(part_keys[2], (CKPTS, TARGETS, K), K ** -0.5, 0.125, ((1, 16),)),
    }


def reference(train_features, residual_weights, target_features):
    raw = jnp.zeros((train_features.shape[1], target_features.shape[1]), jnp.float32)
    for ckpt in range(CKPTS):
        tile = jnp.dot(train_features[ckpt], target_features[ckpt].T, preferred_element_type=jnp.float32)
        raw = raw + residual_weights[ckpt][:, None] * tile
    power = lax.optimization_barrier(jnp.mean(raw * raw, axis=0))
    return (raw / jnp.sqrt(power + 1e-06)[None, :]).astype(jnp.bfloat16)
```

```python
import functools

import jax
import jax.numpy as jnp
from jax import lax
from jax.experimental import pallas as pl
from jax.experimental.pallas import tpu as pltpu
from jax.sharding import PartitionSpec as P

MESH = pl.DeviceIdType.MESH
PIECES = 4
ROW_TILE = 640


def each(low, high, body):
    if high - low <= 16:
        for i in range(low, high):
            body(i)
    else:

        @pl.loop(low, high)
        def _(i):
            body(i)


def kernel(n, train, weights, targets, out, feats, rows, weight_rows, columns, raw, sums,
           own_sem, weight_sem, load_sem, z_send, z_recv, y_send, y_recv, s_send, s_recv,
           sum_send, sum_recv):
    levels = n // 4
    me = lax.axis_index("trn")
    z, y, core = me // 4, (me // 2) % 2, me % 2
    across, sibling = z * 4 + (1 - y) * 2 + core, z * 4 + y * 2 + (1 - core)
    ckpts, count, depth = train.shape
    own = targets.shape[1]
    per_ckpt = PIECES // ckpts
    width = depth // per_ckpt
    where = [(p // per_ckpt, (p % per_ckpt) * width) for p in range(PIECES)]

    def block(zz, yy, cc, p):
        ckpt, start = where[p]
        first = pl.multiple_of((zz * 4 + yy * 2 + cc) * own, own)
        return feats.at[ckpt, pl.ds(first, own), pl.ds(start, width)]

    def piece_rows(blocks, p):
        ckpt, start = where[p]
        return feats.at[ckpt, pl.ds(0, blocks * own), pl.ds(start, width)]

    def remote(ref, device, send_sem, recv_sem):
        return pltpu.make_async_remote_copy(
            src_ref=ref, dst_ref=ref, send_sem=send_sem, recv_sem=recv_sem,
            device_id={"trn": device}, device_id_type=MESH,
        )

    mine = pl.ds(pl.multiple_of(me * own, own), own)
    own_copy = pltpu.make_async_copy(targets, feats.at[:, mine, :], own_sem)
    own_copy.start()
    weight_copy = pltpu.make_async_copy(weights, weight_rows, weight_sem)
    weight_copy.start()
    loads = []
    for p, (ckpt, start) in enumerate(where):
        part = (ckpt, slice(None), pl.ds(start, width))
        loads.append(pltpu.make_async_copy(train.at[part], rows.at[part], load_sem.at[p]))
        loads[-1].start()

    above, below = z + 1 < levels, z > 0
    onward = ((above, me + 4), (below, me - 4))

    barrier = pltpu.get_barrier_semaphore()
    for device in (across, sibling):
        pl.semaphore_signal(barrier, inc=1, device_id={"trn": device}, device_id_type=MESH)
    for there, device in onward:

        @pl.when(there)
        def _():
            pl.semaphore_signal(barrier, inc=1, device_id={"trn": device}, device_id_type=MESH)

    pl.semaphore_wait(barrier, 2 + above.astype(jnp.int32) + below.astype(jnp.int32))
    own_copy.wait()

    def pass_on(way, d, p, ref):
        there, device = onward[way]

        @pl.when(there)
        def _():
            remote(ref, device, z_send.at[way, d, p], z_recv.at[way, d + 1, p]).start()

    def to_across(way, d, p, ref):
        remote(ref, across, y_send.at[p], y_recv.at[way, d, p]).start()

    def to_sibling(p, ref):
        remote(ref, sibling, s_send.at[p], s_recv.at[p]).start()

    for p in range(PIECES):
        ref = block(z, y, core, p)
        pass_on(0, 0, p, ref)
        pass_on(1, 0, p, ref)
        to_across(0, 0, p, ref)
    for p in range(PIECES):
        to_sibling(p, block(z, y, core, p))

    weight_copy.wait()
    for ckpt in range(ckpts):
        for first in range(0, count, 128):
            line = weight_rows[ckpt:ckpt + 1, first:first + 128]
            columns[ckpt, first:first + 128, :] = jnp.broadcast_to(line, (128, 128)).T

    def origin(way, d):
        return z - d if way == 0 else z + d

    def exists(way, d):
        return origin(way, d) >= 0 if way == 0 else origin(way, d) < levels

    def from_z(d, p):
        for way in range(2):

            @pl.when(exists(way, d))
            def _():
                ref = block(origin(way, d), y, core, p)
                remote(ref, me, z_send.at[way, d, p], z_recv.at[way, d, p]).wait_recv()
                pass_on(way, d, p, ref)
                to_across(way, d, p, ref)
                to_sibling(p, ref)

    def from_across(d, p, ways=2):
        for way in range(ways):

            @pl.when(exists(way, d))
            def _():
                ref = block(origin(way, d), 1 - y, core, p)
                remote(ref, me, y_send.at[p], y_recv.at[way, d, p]).wait_recv()
                to_sibling(p, ref)

    def level(d):
        for p in range(PIECES):
            from_z(d, p)
        for p in range(PIECES):
            from_across(d - 1, p)

    if levels > 1:
        for p in range(PIECES):
            from_z(1, p)
        for p in range(PIECES):
            from_across(0, p, ways=1)
        each(2, levels, level)

    targets_all = n * own
    tile = ROW_TILE if count % ROW_TILE == 0 else count
    lanes = targets_all // 128
    squares = jnp.zeros((8, targets_all), jnp.float32)
    for p, (ckpt, start) in enumerate(where):
        from_across(levels - 1, p, ways=2 if levels > 1 else 1)
        remote(piece_rows(2 * levels, p), me, s_send.at[p], s_recv.at[p]).wait_recv()
        loads[p].wait()
        for first in range(0, count, tile):
            here = slice(first, first + tile)
            product = lax.dot_general(
                rows[ckpt, here, start:start + width], feats[ckpt, :, start:start + width],
                (((1,), (1,)), ((), ())), preferred_element_type=jnp.float32,
            )
            scale = jnp.concatenate([columns[ckpt, here, :]] * lanes, axis=1)
            value = product * scale
            if p:
                value += raw[here, :]
            raw[here, :] = value
            if p == PIECES - 1:
                squares += jnp.sum((value * value).reshape(tile // 8, 8, targets_all), axis=0)

    sums[pl.ds(me, 1)] = jnp.sum(squares, axis=0, keepdims=True)[None]

    def send_sum(i):
        device = lax.rem(me + i, n)
        remote(sums.at[pl.ds(me, 1)], device, sum_send, sum_recv).start()

    each(1, n, send_sum)

    for p in range(PIECES):
        remote(piece_rows(levels, p), me, y_send.at[p], y_recv.at[0, 0, p]).wait_send()
        remote(piece_rows(2 * levels, p), me, s_send.at[p], s_recv.at[p]).wait_send()

    def z_sent(d):
        for p in range(PIECES):
            for way in range(2):

                @pl.when(jnp.logical_and(exists(way, d), onward[way][0]))
                def _():
                    ref = block(z, y, core, p)
                    remote(ref, me, z_send.at[way, d, p], z_recv.at[way, d, p]).wait_send()

    each(0, levels, z_sent)

    others = sums.at[pl.ds(0, n - 1)]
    remote(others, me, sum_send, sum_recv).wait_recv()
    power = jnp.sum(sums[...], axis=0) / (count * n)
    inverse = 1.0 / jnp.sqrt(power + 1e-06)
    for first in range(0, count, tile):
        here = slice(first, first + tile)
        out[here, :] = (raw[here, :] * inverse).astype(out.dtype)
    remote(others, me, sum_send, sum_recv).wait_send()


def shards(n, train_features, residual_weights, target_features):
    ckpts, count, depth = train_features.shape
    own = target_features.shape[1]
    dma = pltpu.SemaphoreType.DMA
    levels = n // 4
    return pl.pallas_call(
        functools.partial(kernel, n),
        out_shape=jax.ShapeDtypeStruct((count, n * own), jnp.bfloat16),
        in_specs=[pl.BlockSpec(memory_space=pl.ANY)] * 3,
        out_specs=pl.BlockSpec(memory_space=pltpu.VMEM),
        scratch_shapes=[
            pltpu.VMEM((ckpts, n * own, depth), jnp.bfloat16),
            pltpu.VMEM((ckpts, count, depth), jnp.bfloat16),
            pltpu.VMEM((ckpts, count), jnp.float32),
            pltpu.VMEM((ckpts, count, 128), jnp.float32),
            pltpu.VMEM((count, n * own), jnp.float32),
            pltpu.VMEM((n, 1, n * own), jnp.float32),
            dma, dma, dma((PIECES,)),
            dma((2, levels, PIECES)), dma((2, levels + 1, PIECES)),
            dma((PIECES,)), dma((2, levels, PIECES)),
            dma((PIECES,)), dma((PIECES,)),
            dma, dma,
        ],
        compiler_params=pltpu.CompilerParams(
            collective_id=0, has_side_effects=True, vmem_limit_bytes=56 * 1024 * 1024,
        ),
        cost_estimate=pl.CostEstimate(
            flops=2 * ckpts * count * depth * n * own,
            bytes_accessed=2 * ckpts * count * depth, transcendentals=0,
        ),
    )(train_features, residual_weights, target_features)


def solution(mesh):
    return jax.shard_map(
        functools.partial(shards, mesh.shape["trn"]),
        mesh=mesh,
        in_specs=(
            P(None, ("grp", "trn"), None),
            P(None, ("grp", "trn")),
            P(None, ("grp", "trn"), None),
        ),
        out_specs=P(("grp", "trn"), None),
        check_vma=False,
    )
```

```python
import functools

import jax
import jax.numpy as jnp
from jax import lax
from jax.experimental import pallas as pl
from jax.experimental.pallas import tpu as pltpu
from jax.sharding import PartitionSpec as P

MESH = pl.DeviceIdType.MESH
AHEAD = 2
PIECES = 2
ROW_TILE = 640


def each(low, high, body):
    if high - low <= 16:
        for i in range(low, high):
            body(i)
    else:

        @pl.loop(low, high)
        def _(i):
            body(i)


def kernel(n, train, weights, targets, out, feats, rows, weight_rows, columns, raw, sums,
           own_sem, weight_sem, load_sem, z_send, z_recv, y_send, y_recv, s_send, s_recv,
           sum_send, sum_recv):
    levels = n // 4
    me = lax.axis_index("trn")
    z, y, core = me // 4, (me // 2) % 2, me % 2
    across, sibling = z * 4 + (1 - y) * 2 + core, z * 4 + y * 2 + (1 - core)
    ckpts, count, depth = train.shape
    own = targets.shape[1]
    per_ckpt = PIECES // ckpts
    width = depth // per_ckpt
    where = [(p // per_ckpt, (p % per_ckpt) * width) for p in range(PIECES)]

    def block(zz, yy, p, size=1):
        ckpt, start = where[p]
        return feats.at[ckpt, pl.ds(zz, size), yy, core, :, pl.ds(start, width)]

    def remote(ref, device, send_sem, recv_sem):
        return pltpu.make_async_remote_copy(
            src_ref=ref, dst_ref=ref, send_sem=send_sem, recv_sem=recv_sem,
            device_id={"trn": device}, device_id_type=MESH,
        )

    own_copy = pltpu.make_async_copy(targets, feats.at[:, z, y, core], own_sem)
    own_copy.start()
    weight_copy = pltpu.make_async_copy(weights, weight_rows, weight_sem)
    weight_copy.start()
    loads = []
    for p, (ckpt, start) in enumerate(where):
        part = (ckpt, slice(None), pl.ds(start, width))
        loads.append(pltpu.make_async_copy(train.at[part], rows.at[part], load_sem.at[p]))
        loads[-1].start()

    barrier = pltpu.get_barrier_semaphore()

    def greet(device):
        pl.semaphore_signal(barrier, inc=1, device_id={"trn": device}, device_id_type=MESH)

    above, below = z + 1 < levels, z > 0
    onward = ((above, me + 4), (below, me - 4))
    greet(across)
    greet(sibling)
    for there, device in onward:
        pl.when(there)(functools.partial(greet, device))
    pl.semaphore_wait(barrier, 2 + above.astype(jnp.int32) + below.astype(jnp.int32))
    own_copy.wait()

    def pass_on(way, d, p, ref):
        there, device = onward[way]

        @pl.when(there)
        def _():
            remote(ref, device, z_send.at[way, d, p], z_recv.at[way, d + 1, p]).start()

    def to_across(p, ref):
        remote(ref, across, y_send.at[p], y_recv.at[p]).start()

    def origin(way, d):
        return z - d if way == 0 else z + d

    def exists(way, d):
        return origin(way, d) >= 0 if way == 0 else origin(way, d) < levels

    for p in range(PIECES):
        ref = block(z, y, p)
        pass_on(0, 0, p, ref)
        pass_on(1, 0, p, ref)
        to_across(p, ref)

    weight_copy.wait()
    for ckpt in range(ckpts):
        for first in range(0, count, 128):
            line = weight_rows[ckpt:ckpt + 1, first:first + 128]
            columns[ckpt, first:first + 128, :] = jnp.broadcast_to(line, (128, 128)).T

    def level(d):
        for p in range(PIECES):
            for way in range(2):

                @pl.when(exists(way, d))
                def _():
                    ref = block(origin(way, d), y, p)
                    remote(ref, me, z_send.at[way, d, p], z_recv.at[way, d, p]).wait_recv()
                    pass_on(way, d, p, ref)
                    to_across(p, ref)

    each(1, levels, level)

    def to_sibling(half, p):
        column = block(0, y if half == 0 else 1 - y, p, levels)
        if half:
            remote(column, me, y_send.at[p], y_recv.at[p]).wait_recv()
        remote(column, sibling, s_send.at[half, p], s_recv.at[half, p]).start()

    for p in range(PIECES):
        to_sibling(0, p)
    for p in range(AHEAD):
        to_sibling(1, p)

    targets_all = n * own
    tile = ROW_TILE if count % ROW_TILE == 0 else count
    lanes = targets_all // 128
    squares = jnp.zeros((8, targets_all), jnp.float32)
    for p, (ckpt, start) in enumerate(where):
        if p + AHEAD < PIECES:
            to_sibling(1, p + AHEAD)
        column = block(0, y, p, levels)
        for half in range(2):
            remote(column, me, s_send.at[half, p], s_recv.at[half, p]).wait_recv()
        loads[p].wait()
        for first in range(0, count, tile):
            here = slice(first, first + tile)
            product = lax.dot_general(
                rows[ckpt, here, start:start + width],
                feats[ckpt, :, :, :, :, start:start + width].reshape(targets_all, width),
                (((1,), (1,)), ((), ())), preferred_element_type=jnp.float32,
            )
            scale = jnp.concatenate([columns[ckpt, here, :]] * lanes, axis=1)
            value = product * scale
            if p:
                value += raw[here, :]
            raw[here, :] = value
            if p == PIECES - 1:
                squares += jnp.sum((value * value).reshape(tile // 8, 8, targets_all), axis=0)

    sums[pl.ds(me, 1)] = jnp.sum(squares, axis=0, keepdims=True)[None]

    def send_sum(i):
        device = lax.rem(me + i, n)
        remote(sums.at[pl.ds(me, 1)], device, sum_send, sum_recv).start()

    each(1, n, send_sum)

    for p in range(PIECES):
        column = block(0, y, p, levels)
        remote(column, me, y_send.at[p], y_recv.at[p]).wait_send()
        for half in range(2):
            remote(column, me, s_send.at[half, p], s_recv.at[half, p]).wait_send()

    def z_sent(d):
        for p in range(PIECES):
            for way in range(2):

                @pl.when(jnp.logical_and(exists(way, d), onward[way][0]))
                def _():
                    ref = block(z, y, p)
                    remote(ref, me, z_send.at[way, d, p], z_recv.at[way, d, p]).wait_send()

    each(0, levels, z_sent)

    others = sums.at[pl.ds(0, n - 1)]
    remote(others, me, sum_send, sum_recv).wait_recv()
    power = jnp.sum(sums[...], axis=0) / (count * n)
    inverse = 1.0 / jnp.sqrt(power + 1e-06)
    for first in range(0, count, tile):
        here = slice(first, first + tile)
        out[here, :] = (raw[here, :] * inverse).astype(out.dtype)
    remote(others, me, sum_send, sum_recv).wait_send()


def shards(n, train_features, residual_weights, target_features):
    ckpts, count, depth = train_features.shape
    own = target_features.shape[1]
    dma = pltpu.SemaphoreType.DMA
    levels = n // 4
    return pl.pallas_call(
        functools.partial(kernel, n),
        out_shape=jax.ShapeDtypeStruct((count, n * own), jnp.bfloat16),
        in_specs=[pl.BlockSpec(memory_space=pl.ANY)] * 3,
        out_specs=pl.BlockSpec(memory_space=pltpu.VMEM),
        scratch_shapes=[
            pltpu.VMEM((ckpts, levels, 2, 2, own, depth), jnp.bfloat16),
            pltpu.VMEM((ckpts, count, depth), jnp.bfloat16),
            pltpu.VMEM((ckpts, count), jnp.float32),
            pltpu.VMEM((ckpts, count, 128), jnp.float32),
            pltpu.VMEM((count, n * own), jnp.float32),
            pltpu.VMEM((n, 1, n * own), jnp.float32),
            dma, dma, dma((PIECES,)),
            dma((2, levels, PIECES)), dma((2, levels + 1, PIECES)),
            dma((PIECES,)), dma((PIECES,)),
            dma((2, PIECES)), dma((2, PIECES)),
            dma, dma,
        ],
        compiler_params=pltpu.CompilerParams(
            collective_id=0, has_side_effects=True, vmem_limit_bytes=56 * 1024 * 1024,
        ),
        cost_estimate=pl.CostEstimate(
            flops=2 * ckpts * count * depth * n * own,
            bytes_accessed=2 * ckpts * count * depth, transcendentals=0,
        ),
    )(train_features, residual_weights, target_features)


def solution(mesh):
    return jax.shard_map(
        functools.partial(shards, mesh.shape["trn"]),
        mesh=mesh,
        in_specs=(
            P(None, ("grp", "trn"), None),
            P(None, ("grp", "trn")),
            P(None, ("grp", "trn"), None),
        ),
        out_specs=P(("grp", "trn"), None),
        check_vma=False,
    )
```

```python
import functools

import jax
import jax.numpy as jnp
from jax import lax
from jax.experimental import pallas as pl
from jax.experimental.pallas import tpu as pltpu
from jax.sharding import PartitionSpec as P

MESH = pl.DeviceIdType.MESH
AHEAD = 2
PIECES = 2
ROW_TILE = 640


def each(low, high, body):
    if high - low <= 16:
        for i in range(low, high):
            body(i)
    else:

        @pl.loop(low, high)
        def _(i):
            body(i)


def kernel(n, train, weights, targets, out, feats, rows, weight_rows, columns, raw, sums,
           own_sem, weight_sem, load_sem, z_send, z_recv, y_send, y_recv, s_send, s_recv,
           sum_send, sum_recv):
    levels = n // 4
    me = lax.axis_index("trn")
    z, y, core = me // 4, (me // 2) % 2, me % 2
    across, sibling = z * 4 + (1 - y) * 2 + core, z * 4 + y * 2 + (1 - core)
    ckpts, count, depth = train.shape
    own = targets.shape[1]
    per_ckpt = PIECES // ckpts
    width = depth // per_ckpt
    where = [(p // per_ckpt, (p % per_ckpt) * width) for p in range(PIECES)]

    def block(zz, yy, p, size=1):
        ckpt, start = where[p]
        return feats.at[ckpt, pl.ds(zz, size), yy, core, :, pl.ds(start, width)]

    def remote(ref, device, send_sem, recv_sem):
        return pltpu.make_async_remote_copy(
            src_ref=ref, dst_ref=ref, send_sem=send_sem, recv_sem=recv_sem,
            device_id={"trn": device}, device_id_type=MESH,
        )

    own_copy = pltpu.make_async_copy(targets, feats.at[:, z, y, core], own_sem)
    own_copy.start()
    weight_copy = pltpu.make_async_copy(weights, weight_rows, weight_sem)
    weight_copy.start()
    loads = []
    for p, (ckpt, start) in enumerate(where):
        part = (ckpt, slice(None), pl.ds(start, width))
        loads.append(pltpu.make_async_copy(train.at[part], rows.at[part], load_sem.at[p]))
        loads[-1].start()

    barrier = pltpu.get_barrier_semaphore()

    def greet(device):
        pl.semaphore_signal(barrier, inc=1, device_id={"trn": device}, device_id_type=MESH)

    above, below = z + 1 < levels, z > 0
    onward = ((above, me + 4), (below, me - 4))
    greet(across)
    greet(sibling)
    for there, device in onward:
        pl.when(there)(functools.partial(greet, device))
    pl.semaphore_wait(barrier, 2 + above.astype(jnp.int32) + below.astype(jnp.int32))
    own_copy.wait()

    def pass_on(way, d, p, ref):
        there, device = onward[way]

        @pl.when(there)
        def _():
            remote(ref, device, z_send.at[way, d, p], z_recv.at[way, d + 1, p]).start()

    def to_across(p, ref):
        remote(ref, across, y_send.at[p], y_recv.at[p]).start()

    def origin(way, d):
        return z - d if way == 0 else z + d

    def exists(way, d):
        return origin(way, d) >= 0 if way == 0 else origin(way, d) < levels

    for p in range(PIECES):
        ref = block(z, y, p)
        pass_on(0, 0, p, ref)
        pass_on(1, 0, p, ref)
        to_across(p, ref)

    weight_copy.wait()
    for ckpt in range(ckpts):
        for first in range(0, count, 128):
            line = weight_rows[ckpt:ckpt + 1, first:first + 128]
            columns[ckpt, first:first + 128, :] = jnp.broadcast_to(line, (128, 128)).T

    def level(d):
        for p in range(PIECES):
            for way in range(2):

                @pl.when(exists(way, d))
                def _():
                    ref = block(origin(way, d), y, p)
                    remote(ref, me, z_send.at[way, d, p], z_recv.at[way, d, p]).wait_recv()
                    pass_on(way, d, p, ref)
                    to_across(p, ref)

    each(1, levels, level)

    def to_sibling(half, p):
        column = block(0, y if half == 0 else 1 - y, p, levels)
        if half:
            remote(column, me, y_send.at[p], y_recv.at[p]).wait_recv()
        remote(column, sibling, s_send.at[half, p], s_recv.at[half, p]).start()

    for p in range(PIECES):
        to_sibling(0, p)
    for p in range(AHEAD):
        to_sibling(1, p)

    targets_all = n * own
    tile = ROW_TILE if count % ROW_TILE == 0 else count
    lanes = targets_all // 128
    squares = jnp.zeros((8, targets_all), jnp.float32)
    for p, (ckpt, start) in enumerate(where):
        if p + AHEAD < PIECES:
            to_sibling(1, p + AHEAD)
        column = block(0, y, p, levels)
        for half in range(2):
            remote(column, me, s_send.at[half, p], s_recv.at[half, p]).wait_recv()
        loads[p].wait()
        for first in range(0, count, tile):
            here = slice(first, first + tile)
            product = lax.dot_general(
                rows[ckpt, here, start:start + width],
                feats[ckpt, :, :, :, :, start:start + width].reshape(targets_all, width),
                (((1,), (1,)), ((), ())), preferred_element_type=jnp.float32,
            )
            scale = jnp.concatenate([columns[ckpt, here, :]] * lanes, axis=1)
            value = product * scale
            if p:
                value += raw[here, :]
            raw[here, :] = value
            if p == PIECES - 1:
                squares += jnp.sum((value * value).reshape(tile // 8, 8, targets_all), axis=0)

    sums[pl.ds(me, 1)] = jnp.sum(squares, axis=0, keepdims=True)[None]

    def send_sum(i):
        device = lax.rem(me + i, n)
        remote(sums.at[pl.ds(me, 1)], device, sum_send, sum_recv).start()

    each(1, n, send_sum)

    for p in range(PIECES):
        column = block(0, y, p, levels)
        remote(column, me, y_send.at[p], y_recv.at[p]).wait_send()
        for half in range(2):
            remote(column, me, s_send.at[half, p], s_recv.at[half, p]).wait_send()

    def z_sent(d):
        for p in range(PIECES):
            for way in range(2):

                @pl.when(jnp.logical_and(exists(way, d), onward[way][0]))
                def _():
                    ref = block(z, y, p)
                    remote(ref, me, z_send.at[way, d, p], z_recv.at[way, d, p]).wait_send()

    each(0, levels, z_sent)

    others = sums.at[pl.ds(0, n - 1)]
    remote(others, me, sum_send, sum_recv).wait_recv()
    power = jnp.sum(sums[...], axis=0) / (count * n)
    inverse = 1.0 / jnp.sqrt(power + 1e-06)
    for first in range(0, count, tile):
        here = slice(first, first + tile)
        out[here, :] = (raw[here, :] * inverse).astype(out.dtype)
    remote(others, me, sum_send, sum_recv).wait_send()


def shards(n, train_features, residual_weights, target_features):
    ckpts, count, depth = train_features.shape
    own = target_features.shape[1]
    dma = pltpu.SemaphoreType.DMA
    levels = n // 4
    return pl.pallas_call(
        functools.partial(kernel, n),
        out_shape=pltpu.VMEM((count, n * own), jnp.bfloat16),
        in_specs=[pl.BlockSpec(memory_space=pl.ANY)] * 3,
        out_specs=pl.BlockSpec(memory_space=pltpu.VMEM),
        scratch_shapes=[
            pltpu.VMEM((ckpts, levels, 2, 2, own, depth), jnp.bfloat16),
            pltpu.VMEM((ckpts, count, depth), jnp.bfloat16),
            pltpu.VMEM((ckpts, count), jnp.float32),
            pltpu.VMEM((ckpts, count, 128), jnp.float32),
            pltpu.VMEM((count, n * own), jnp.float32),
            pltpu.VMEM((n, 1, n * own), jnp.float32),
            dma, dma, dma((PIECES,)),
            dma((2, levels, PIECES)), dma((2, levels + 1, PIECES)),
            dma((PIECES,)), dma((PIECES,)),
            dma((2, PIECES)), dma((2, PIECES)),
            dma, dma,
        ],
        compiler_params=pltpu.CompilerParams(
            collective_id=0, has_side_effects=True, vmem_limit_bytes=56 * 1024 * 1024,
        ),
        cost_estimate=pl.CostEstimate(
            flops=2 * ckpts * count * depth * n * own,
            bytes_accessed=2 * ckpts * count * depth, transcendentals=0,
        ),
    )(train_features, residual_weights, target_features)


def solution(mesh):
    return jax.shard_map(
        functools.partial(shards, mesh.shape["trn"]),
        mesh=mesh,
        in_specs=(
            P(None, ("grp", "trn"), None),
            P(None, ("grp", "trn")),
            P(None, ("grp", "trn"), None),
        ),
        out_specs=P(("grp", "trn"), None),
        check_vma=False,
    )
```
